32 devices in a mesh: tm: 4 (over z), row: 4 (over y, core), col: 2 (over x).
Axes of the slice: x: 2, y: 2, z: 4, core: 2. Of those that a mesh axis runs over, the one named last changes fastest.
Arguments:
- frames: float32 [4, 1024, 1024], P('tm', 'row', 'col'), may hold values from 0 to 200, as said below
- following: float32 [1024, 1024], P('row', 'col'), may hold values from 0 to 200, as said below
Outputs:
- planes: float32 [4, 32, 64, 2048], P('tm', 'row', None, 'col')
The draws below stay inside these ranges and needn't reach their ends.
Inputs may be any that keep to these rules, and one draw needn't show every extreme that they name: `frames`: detector intensities, never negative. `following`: detector intensities, never negative.
All inputs are finite; a program needn't handle non-finite values.
Results may differ from the reference program's by a relative error of at most 0.000071.
Values sent between devices are 32-bit elements; how exact they have to be, the bound alone decides.
A program may use at most 128 MiB of HBM per device.

```python
import math
import jax
import jax.numpy as jnp
from jax import lax

W = 64
STRIDE = 32
FRAMES = 4
NROWS = 1024
NCOLS = 1024


def speckle(key, frame_total):
    grain_key = jax.random.fold_in(key, 0)
    row_key = jax.random.fold_in(key, 2)
    col_key = jax.random.fold_in(key, 3)
    grains = jnp.minimum(jax.random.exponential(grain_key, (frame_total, NROWS, NCOLS), jnp.float32), 12.0)
    log_span = math.log(10.0)
    row_gain = jnp.exp(log_span * jax.random.uniform(row_key, (frame_total, NROWS, 1), jnp.float32))
    col_gain = jnp.exp(log_span * jax.random.uniform(col_key, (frame_total, 1, NCOLS), jnp.float32))
    return grains * row_gain * col_gain / math.exp(log_span)


def draw_frames(key, part):
    return speckle(jax.random.fold_in(key, 11), FRAMES)


def draw_following(key, part):
    return speckle(jax.random.fold_in(key, 23), 1)[0]


def setup_inputs(seed: int = 0) -> dict:
    key_list = jax.random.split(jax.random.key(seed), 3)
    frames = draw_frames(jax.random.fold_in(key_list[2], 71), 0)
    following = draw_following(jax.random.fold_in(key_list[2], 71), 0)
    return dict(frames=frames, following=following)


def cut_windows(frame):
    padded = jnp.pad(frame, ((0, STRIDE), (0, STRIDE)))
    blocks = padded.reshape(NROWS // STRIDE + 1, STRIDE, NCOLS // STRIDE + 1, STRIDE)
    row_pairs = jnp.concatenate([blocks[:-1], blocks[1:]], axis=1)
    windows = jnp.concatenate([row_pairs[:, :, :-1], row_pairs[:, :, 1:]], axis=3)
    centred = windows - lax.optimization_barrier(jnp.mean(windows, axis=(1, 3), keepdims=True))
    spread = lax.optimization_barrier(jnp.mean(centred * centred, axis=(1, 3), keepdims=True))
    return centred * lax.rsqrt(spread + 1e-05)

def pair_planes(pair):
    current, upcoming = pair
    first = jnp.fft.fft2(cut_windows(current), axes=(1, 3))
    second = jnp.fft.fft2(cut_windows(upcoming), axes=(1, 3))
    summed = jnp.real(jnp.fft.ifft2(jnp.conj(first) * second, axes=(1, 3))) / W
    return summed.reshape(NROWS // STRIDE, W, NCOLS // STRIDE * W).astype(jnp.float32)

def reference(frames, following):
    upcoming = jnp.concatenate([frames[1:], following[None]], axis=0)
    return lax.map(pair_planes, (frames, upcoming))
```

```python
import functools

import jax
import jax.numpy as jnp
import ml_dtypes
import numpy as np
from jax import lax
from jax.experimental import pallas as pl
from jax.experimental.pallas import tpu as pltpu
from jax.sharding import PartitionSpec as P

W = 64
HALF = W // 2
STRIDE = 32
LANES = 128
GROUP = 256
PER = GROUP // W
MESH = pl.DeviceIdType.MESH
BF16 = jnp.bfloat16
F32 = jnp.float32


def halves(table):
    high = table.astype(ml_dtypes.bfloat16)
    low = (table - high.astype(np.float64)).astype(ml_dtypes.bfloat16)
    return high, low


def tables():
    angle = 2 * np.pi * (np.outer(np.arange(W), np.arange(HALF + 1)) % W) / W
    cosine, sine = np.cos(angle), np.sin(angle)
    packed = np.concatenate([cosine[:, :HALF], cosine[:, HALF:], sine[:, 1:HALF]], axis=1)
    sign = np.where(np.arange(W) > HALF, -1.0, 1.0)
    weight = np.where(np.arange(W) % HALF == 0, 1.0, 2.0)
    forward_lanes = np.zeros((GROUP, GROUP))
    inverse_lanes = np.zeros((GROUP, GROUP))
    ones = np.zeros((GROUP, GROUP))
    for w in range(PER):
        cells = slice(w * W, w * W + W)
        ones[cells, cells] = 1.0
        for part in range(2):
            slots = slice(part * HALF, part * HALF + HALF)
            place = slice(part * LANES + w * HALF, part * LANES + w * HALF + HALF)
            forward_lanes[cells, place] = (packed * sign)[:, slots]
            inverse_lanes[place, cells] = (packed * weight)[:, slots].T
    square = np.stack(
        [*halves(forward_lanes), *halves(inverse_lanes), ones.astype(ml_dtypes.bfloat16)]
    )
    down, up = packed.T, packed * weight / float(W * W * W)
    tall = []
    for table in (down, up):
        high, low = halves(table)
        tall.append(np.concatenate([high, low, high, low], axis=1))
    return square, np.stack(tall)


def split(x):
    high = x.astype(BF16)
    return high, (x - high.astype(F32)).astype(BF16)


def dot(a, b):
    return jnp.dot(a, b, preferred_element_type=F32)


def expand(block):
    count = block.shape[1] // LANES - 1
    lane = lax.broadcasted_iota(jnp.int32, (W, LANES), 1)
    out = []
    for n in range(count):
        here = block[:, n * LANES : (n + 1) * LANES]
        after = block[:, (n + 1) * LANES : (n + 2) * LANES]
        out.append(jnp.where(lane < W, here, pltpu.roll(here, STRIDE, 1)))
        mixed = jnp.where(lane >= LANES - STRIDE, here, after)
        out.append(
            jnp.where(lane < W, pltpu.roll(here, W, 1), pltpu.roll(mixed, LANES - STRIDE, 1))
        )
    return jnp.concatenate(out, axis=1)


def group_sums(columns, ones):
    groups = columns[0].shape[1] // GROUP
    tall = jnp.concatenate(
        [c[:, g * GROUP : (g + 1) * GROUP] for c in columns for g in range(groups)], axis=0
    )
    high, rest = tall.astype(BF16), None
    rest = tall - high.astype(F32)
    mid, low = split(rest)
    rows = tall.shape[0]
    sums = dot(jnp.concatenate([high, mid, low], axis=0), ones)
    sums = sums[:rows] + sums[rows : 2 * rows] + sums[2 * rows :]
    out = []
    for c in range(len(columns)):
        parts = [sums[(c * groups + g) * 8 : (c * groups + g) * 8 + 8] for g in range(groups)]
        out.append(jnp.sum(jnp.concatenate(parts, axis=1), axis=0, keepdims=True))
    return out


def fold(x):
    return jnp.sum(x.reshape(W // 8, 8, x.shape[1]), axis=0)


def stack_groups(arrays):
    return jnp.concatenate(
        [
            a[:, g * GROUP : (g + 1) * GROUP]
            for a in arrays
            for g in range(a.shape[1] // GROUP)
        ],
        axis=0,
    )


def unstack_groups(tall, count):
    groups = tall.shape[0] // (count * W)
    return [
        jnp.concatenate(
            [tall[(c * groups + g) * W : (c * groups + g + 1) * W] for g in range(groups)], axis=1
        )
        for c in range(count)
    ]


def by_lanes(arrays, high_table, low_table):
    high, low = split(stack_groups(arrays))
    rows = high.shape[0]
    both = dot(jnp.concatenate([high, low], axis=0), high_table)
    tall = both[:rows] + both[rows:] + dot(high, low_table)
    return unstack_groups(tall, len(arrays))


def by_rows(x, table):
    high, low = split(x)
    return dot(table, jnp.concatenate([high, high, low, low], axis=0))


def forward(blocks, square, tall):
    windows = [expand(b) for b in blocks]
    means = group_sums([fold(w) for w in windows], square[4])
    centred = [w - m * (1.0 / (W * W)) for w, m in zip(windows, means)]
    spreads = group_sums([fold(c * c) for c in centred], square[4])
    scales = [lax.rsqrt(s * (1.0 / (W * W)) + 1e-05) for s in spreads]
    rows = by_lanes(centred, square[0], square[1])
    return [by_rows(r, tall[0]) for r in rows], scales


def multiply(x1, x2):
    row = lax.broadcasted_iota(jnp.int32, (HALF, LANES), 0)
    lane = lax.broadcasted_iota(jnp.int32, (HALF, LANES), 1)
    mk = row == 0
    ml = lax.rem(lane, HALF) == 0
    either, both = mk | ml, mk & ml
    top, bottom = [], []
    for g in range(x1.shape[1] // GROUP):
        real, imag = slice(g * GROUP, g * GROUP + LANES), slice(g * GROUP + LANES, (g + 1) * GROUP)
        a1, c1, d1, b1 = x1[:HALF, real], x1[:HALF, imag], x1[HALF:, real], x1[HALF:, imag]
        a2, c2, d2, b2 = x2[:HALF, real], x2[:HALF, imag], x2[HALF:, real], x2[HALF:, imag]
        bb, cc, dd = b1 * b2, c1 * c2, d1 * d2
        cb_bc, bd_db = c1 * b2 - b1 * c2, b1 * d2 - d1 * b2
        top.append(
            a1 * a2 + jnp.where(ml, 0.0, cc) + jnp.where(mk, 0.0, dd) + jnp.where(either, 0.0, bb)
        )
        top.append(
            jnp.where(ml, cc, c1 * a2 - a1 * c2) + jnp.where(mk, 0.0, jnp.where(ml, bb, bd_db))
        )
        bottom.append(
            jnp.where(mk, dd, a1 * d2 - d1 * a2) + jnp.where(ml, 0.0, jnp.where(mk, bb, cb_bc))
        )
        inner = c1 * d2 + d1 * c2 - a1 * b2 - b1 * a2
        bottom.append(
            jnp.where(both, bb, jnp.where(ml, cb_bc, jnp.where(mk, bd_db, inner)))
        )
    return jnp.concatenate(
        [jnp.concatenate(top, axis=1), jnp.concatenate(bottom, axis=1)], axis=0
    )


def inverse(powers, square, tall):
    return by_lanes([by_rows(p, tall[1]) for p in powers], square[2], square[3])


def kernel(
    sizes, frames, following, square_in, tall_in, out,
    ext, spec, scale, result, square, tall, local_sem, send_sem, recv_sem, out_sem,
):
    F, H, B = frames.shape
    rows = H // STRIDE
    pairs = rows // 2
    tm, row, col = (lax.axis_index(a) for a in ("tm", "row", "col"))
    last_tm, last_row, last_col = (s - 1 for s in sizes)
    has_next, has_prev = tm < last_tm, tm > 0
    has_below, has_above = row < last_row, row > 0
    has_right, has_left = col < last_col, col > 0
    up, left, back = (jnp.maximum(v - 1, 0) for v in (row, col, tm))
    down, right, ahead = (
        jnp.minimum(v + 1, s) for v, s in ((row, last_row), (col, last_col), (tm, last_tm))
    )

    own = pltpu.make_async_copy(frames, ext.at[pl.ds(0, F), pl.ds(0, H), pl.ds(0, B)], local_sem.at[0])
    own.start()
    after = pltpu.make_async_copy(following, ext.at[F, pl.ds(0, H), pl.ds(0, B)], local_sem.at[1])
    pl.when(~has_next)(after.start)
    load_square = pltpu.make_async_copy(square_in, square, local_sem.at[2])
    load_square.start()
    load_tall = pltpu.make_async_copy(tall_in, tall, local_sem.at[3])
    load_tall.start()

    neighbours = [
        (has_prev, (back, row, col)),
        (has_next, (ahead, row, col)),
        (has_above, (tm, up, col)),
        (has_below, (tm, down, col)),
        (has_left, (tm, row, left)),
        (has_right, (tm, row, right)),
        (has_above & has_left, (tm, up, left)),
        (has_below & has_right, (tm, down, right)),
    ]
    barrier = pltpu.get_barrier_semaphore()
    for there, device in neighbours:
        @pl.when(there)
        def _(device=device):
            pl.semaphore_signal(barrier, inc=1, device_id=device, device_id_type=MESH)
    pl.semaphore_wait(barrier, sum(there.astype(jnp.int32) for there, _ in neighbours))

    def remote(source, target, number, device):
        return pltpu.make_async_remote_copy(
            src_ref=source, dst_ref=target, send_sem=send_sem.at[number],
            recv_sem=recv_sem.at[number], device_id=device, device_id_type=MESH,
        )

    strip = remote(
        frames.at[0, :, pl.ds(0, LANES)], ext.at[F, pl.ds(0, H), pl.ds(0, LANES)], 0, (back, row, col)
    )
    edges = [0, STRIDE] + [STRIDE + W * (p + 1) for p in range(pairs - 1)] + [H]
    wide = pl.ds(LANES, B - LANES)
    bands = [
        remote(
            frames.at[0, pl.ds(lo, hi - lo), wide], ext.at[F, pl.ds(lo, hi - lo), wide],
            1 + n, (back, row, col),
        )
        for n, (lo, hi) in enumerate(zip(edges[:-1], edges[1:]))
    ]
    base = 1 + len(bands)
    rim_rows, rim_cols = pl.ds(H, STRIDE), pl.ds(B, LANES)
    first, everyone = pl.ds(0, LANES), pl.ds(0, F)
    rims = [
        (has_left, has_right, remote(
            frames.at[:, :, first], ext.at[everyone, pl.ds(0, H), rim_cols],
            base, (tm, row, left))),
        (has_above, has_below, remote(
            frames.at[:, pl.ds(0, STRIDE), :], ext.at[everyone, rim_rows, pl.ds(0, B)],
            base + 1, (tm, up, col))),
        (has_above & has_left, has_below & has_right, remote(
            frames.at[:, pl.ds(0, STRIDE), first], ext.at[everyone, rim_rows, rim_cols],
            base + 2, (tm, up, left))),
    ]
    late = [
        (has_left, has_right, remote(
            ext.at[F, pl.ds(0, H), first], ext.at[F, pl.ds(0, H), rim_cols],
            base + 3, (tm, row, left))),
        (has_above & has_left, has_below & has_right, remote(
            ext.at[F, pl.ds(0, STRIDE), first], ext.at[F, rim_rows, rim_cols],
            base + 4, (tm, up, left))),
        (has_above, has_below, remote(
            ext.at[F, pl.ds(0, STRIDE), pl.ds(0, B)], ext.at[F, rim_rows, pl.ds(0, B)],
            base + 5, (tm, up, col))),
    ]

    @pl.when(has_prev)
    def _():
        strip.start()
        for band in bands:
            band.start()
    for sends, _, copy in rims:
        pl.when(sends)(copy.start)

    @pl.when(~has_right)
    def _():
        ext[:, :, pl.ds(B, LANES)] = jnp.zeros((F + 1, H + STRIDE, LANES), F32)

    @pl.when(~has_below)
    def _():
        ext[:, pl.ds(H, STRIDE), :] = jnp.zeros((F + 1, STRIDE, B + LANES), F32)

    load_square.wait()
    load_tall.wait()
    own.wait()
    for _, comes, copy in rims:
        pl.when(comes)(copy.wait_recv)

    def spectra(frame, p):
        blocks = []
        for r in range(2):
            start = pl.multiple_of((2 * p + r) * STRIDE, STRIDE)
            blocks.append(ext[frame, pl.ds(start, W), :])
        return forward(blocks, square, tall)

    def keep(slot, p, found):
        for r in range(2):
            spec[slot, 2 * p + r] = found[0][r]
            scale[slot, 2 * p + r] = jnp.broadcast_to(found[1][r], scale.shape[2:])

    def emit(frame, slot, p, found):
        powers = [multiply(spec[slot, 2 * p + r], found[0][r]) for r in range(2)]
        planes = inverse(powers, square, tall)
        for r in range(2):
            factor = found[1][r] * scale[slot, 2 * p + r][:1]
            result[frame, 2 * p + r] = planes[r] * factor

    def to_out(frame, p):
        part = pl.ds(2 * p, 2)
        return pltpu.make_async_copy(
            result.at[frame, part], out.at[frame, part], out_sem.at[frame, p]
        )

    @pl.loop(0, pairs)
    def _(p):
        keep(0, p, spectra(0, p))

    for f in range(1, F):
        @pl.loop(0, pairs)
        def _(p):
            found = spectra(f, p)
            emit(f - 1, (f - 1) % 2, p, found)
            keep(f % 2, p, found)
            to_out(f - 1, p).start()

    @pl.when(has_next)
    def _():
        strip.wait_recv()
        bands[0].wait_recv()

    pl.when(~has_next)(after.wait)
    for sends, _, copy in late:
        pl.when(sends)(copy.start)
    for _, comes, copy in late[:1]:
        pl.when(comes)(copy.wait_recv)
    for p in range(pairs):
        pl.when(has_next)(bands[p + 1].wait_recv)
        if p == pairs - 1:
            for _, comes, copy in late[1:]:
                pl.when(comes)(copy.wait_recv)
        emit(F - 1, (F - 1) % 2, p, spectra(F, p))
        to_out(F - 1, p).start()

    @pl.when(has_prev)
    def _():
        strip.wait_send()
        for band in bands:
            band.wait_send()
    for sends, _, copy in rims + late:
        pl.when(sends)(copy.wait_send)
    for f in range(F):
        for p in range(pairs):
            to_out(f, p).wait()


def on_device(sizes, frames, following):
    F, H, B = frames.shape
    rows, lanes = H // STRIDE, B // STRIDE * W
    square, tall = tables()
    copies = 1 + rows // 2 + 1 + 6
    return pl.pallas_call(
        functools.partial(kernel, sizes),
        out_shape=jax.ShapeDtypeStruct((F, rows, W, lanes), F32),
        in_specs=[pl.BlockSpec(memory_space=pl.ANY)] * 4,
        out_specs=pl.BlockSpec(memory_space=pl.ANY),
        scratch_shapes=[
            pltpu.VMEM((F + 1, H + STRIDE, B + LANES), F32),
            pltpu.VMEM((2, rows, W, lanes), F32),
            pltpu.VMEM((2, rows, 8, lanes), F32),
            pltpu.VMEM((F, rows, W, lanes), F32),
            pltpu.VMEM(square.shape, BF16),
            pltpu.VMEM(tall.shape, BF16),
            pltpu.SemaphoreType.DMA((4,)),
            pltpu.SemaphoreType.DMA((copies,)),
            pltpu.SemaphoreType.DMA((copies,)),
            pltpu.SemaphoreType.DMA((F, rows // 2)),
        ],
        compiler_params=pltpu.CompilerParams(
            collective_id=0, has_side_effects=True, vmem_limit_bytes=40 * 1024 * 1024
        ),
    )(frames, following, jnp.asarray(square), jnp.asarray(tall))


def solution(mesh):
    sizes = tuple(mesh.shape[a] for a in ("tm", "row", "col"))
    return jax.shard_map(
        functools.partial(on_device, sizes),
        mesh=mesh,
        in_specs=(P("tm", "row", "col"), P("row", "col")),
        out_specs=P("tm", "row", None, "col"),
        check_vma=False,
    )
```

```python
import functools

import jax
import jax.numpy as jnp
import ml_dtypes
import numpy as np
from jax import lax
from jax.experimental import pallas as pl
from jax.experimental.pallas import tpu as pltpu
from jax.sharding import PartitionSpec as P

W = 64
HALF = W // 2
STRIDE = 32
LANES = 128
GROUP = 256
PER = GROUP // W
DEPTH = 2
MESH = pl.DeviceIdType.MESH
BF16 = jnp.bfloat16
F32 = jnp.float32


def halves(table):
    high = table.astype(ml_dtypes.bfloat16)
    low = (table - high.astype(np.float64)).astype(ml_dtypes.bfloat16)
    return high, low


def tables():
    angle = 2 * np.pi * (np.outer(np.arange(W), np.arange(HALF + 1)) % W) / W
    cosine, sine = np.cos(angle), np.sin(angle)
    packed = np.concatenate([cosine[:, :HALF], cosine[:, HALF:], sine[:, 1:HALF]], axis=1)
    sign = np.where(np.arange(W) > HALF, -1.0, 1.0)
    weight = np.where(np.arange(W) % HALF == 0, 1.0, 2.0)
    forward_lanes = np.zeros((GROUP, GROUP))
    inverse_lanes = np.zeros((GROUP, GROUP))
    ones = np.zeros((GROUP, GROUP))
    for w in range(PER):
        cells = slice(w * W, w * W + W)
        ones[cells, cells] = 1.0
        for part in range(2):
            slots = slice(part * HALF, part * HALF + HALF)
            place = slice(part * LANES + w * HALF, part * LANES + w * HALF + HALF)
            forward_lanes[cells, place] = (packed * sign)[:, slots]
            inverse_lanes[place, cells] = (packed * weight)[:, slots].T
    square = np.stack(
        [*halves(forward_lanes), *halves(inverse_lanes), ones.astype(ml_dtypes.bfloat16)]
    )
    down, up = packed.T, packed * weight / float(W * W * W)
    tall = []
    for table in (down, up):
        high, low = halves(table)
        tall.append(np.concatenate([high, low, high, low], axis=1))
    return square, np.stack(tall)


def split(x):
    high = x.astype(BF16)
    return high, (x - high.astype(F32)).astype(BF16)


def dot(a, b):
    return jnp.dot(a, b, preferred_element_type=F32)


def pack(columns):
    lane = lax.broadcasted_iota(jnp.int32, (8, LANES), 1)
    out = []
    for top in range(0, columns.shape[0], STRIDE):
        tiles = [columns[top + 8 * b : top + 8 * b + 8] for b in range(4)]
        tile = tiles[0]
        for b in range(1, 4):
            tile = jnp.where(lane < b * STRIDE, tile, pltpu.roll(tiles[b], b * STRIDE, 1))
        out.append(tile)
    return jnp.concatenate(out, axis=0)


def unpack(packed):
    out = []
    for top in range(0, packed.shape[0], 8):
        tile = packed[top : top + 8]
        out.append(tile)
        out += [pltpu.roll(tile, LANES - b * STRIDE, 1) for b in range(1, 4)]
    return jnp.concatenate(out, axis=0)


def expand(block):
    count = block.shape[1] // LANES - 1
    lane = lax.broadcasted_iota(jnp.int32, (W, LANES), 1)
    out = []
    for n in range(count):
        here = block[:, n * LANES : (n + 1) * LANES]
        after = block[:, (n + 1) * LANES : (n + 2) * LANES]
        out.append(jnp.where(lane < W, here, pltpu.roll(here, STRIDE, 1)))
        mixed = jnp.where(lane >= LANES - STRIDE, here, after)
        out.append(
            jnp.where(lane < W, pltpu.roll(here, W, 1), pltpu.roll(mixed, LANES - STRIDE, 1))
        )
    return jnp.concatenate(out, axis=1)


def group_sums(columns, ones):
    groups = columns[0].shape[1] // GROUP
    tall = jnp.concatenate(
        [c[:, g * GROUP : (g + 1) * GROUP] for c in columns for g in range(groups)], axis=0
    )
    high, rest = tall.astype(BF16), None
    rest = tall - high.astype(F32)
    mid, low = split(rest)
    rows = tall.shape[0]
    sums = dot(jnp.concatenate([high, mid, low], axis=0), ones)
    sums = sums[:rows] + sums[rows : 2 * rows] + sums[2 * rows :]
    out = []
    for c in range(len(columns)):
        parts = [sums[(c * groups + g) * 8 : (c * groups + g) * 8 + 8] for g in range(groups)]
        out.append(jnp.sum(jnp.concatenate(parts, axis=1), axis=0, keepdims=True))
    return out


def fold(x):
    return jnp.sum(x.reshape(W // 8, 8, x.shape[1]), axis=0)


def stack_groups(arrays):
    return jnp.concatenate(
        [
            a[:, g * GROUP : (g + 1) * GROUP]
            for a in arrays
            for g in range(a.shape[1] // GROUP)
        ],
        axis=0,
    )


def unstack_groups(tall, count):
    groups = tall.shape[0] // (count * W)
    return [
        jnp.concatenate(
            [tall[(c * groups + g) * W : (c * groups + g + 1) * W] for g in range(groups)], axis=1
        )
        for c in range(count)
    ]


def by_lanes(arrays, high_table, low_table):
    high, low = split(stack_groups(arrays))
    rows = high.shape[0]
    both = dot(jnp.concatenate([high, low], axis=0), high_table)
    tall = both[:rows] + both[rows:] + dot(high, low_table)
    return unstack_groups(tall, len(arrays))


def by_rows(x, table):
    high, low = split(x)
    return dot(table, jnp.concatenate([high, high, low, low], axis=0))


def forward(blocks, square, tall):
    windows = [expand(b) for b in blocks]
    means = group_sums([fold(w) for w in windows], square[4])
    centred = [w - m * (1.0 / (W * W)) for w, m in zip(windows, means)]
    spreads = group_sums([fold(c * c) for c in centred], square[4])
    scales = [lax.rsqrt(s * (1.0 / (W * W)) + 1e-05) for s in spreads]
    rows = by_lanes(centred, square[0], square[1])
    return [by_rows(r, tall[0]) for r in rows], scales


def multiply(x1, x2):
    row = lax.broadcasted_iota(jnp.int32, (HALF, LANES), 0)
    lane = lax.broadcasted_iota(jnp.int32, (HALF, LANES), 1)
    mk = row == 0
    ml = lax.rem(lane, HALF) == 0
    either, both = mk | ml, mk & ml
    top, bottom = [], []
    for g in range(x1.shape[1] // GROUP):
        real, imag = slice(g * GROUP, g * GROUP + LANES), slice(g * GROUP + LANES, (g + 1) * GROUP)
        a1, c1, d1, b1 = x1[:HALF, real], x1[:HALF, imag], x1[HALF:, real], x1[HALF:, imag]
        a2, c2, d2, b2 = x2[:HALF, real], x2[:HALF, imag], x2[HALF:, real], x2[HALF:, imag]
        bb, cc, dd = b1 * b2, c1 * c2, d1 * d2
        cb_bc, bd_db = c1 * b2 - b1 * c2, b1 * d2 - d1 * b2
        top.append(
            a1 * a2 + jnp.where(ml, 0.0, cc) + jnp.where(mk, 0.0, dd) + jnp.where(either, 0.0, bb)
        )
        top.append(
            jnp.where(ml, cc, c1 * a2 - a1 * c2) + jnp.where(mk, 0.0, jnp.where(ml, bb, bd_db))
        )
        bottom.append(
            jnp.where(mk, dd, a1 * d2 - d1 * a2) + jnp.where(ml, 0.0, jnp.where(mk, bb, cb_bc))
        )
        inner = c1 * d2 + d1 * c2 - a1 * b2 - b1 * a2
        bottom.append(
            jnp.where(both, bb, jnp.where(ml, cb_bc, jnp.where(mk, bd_db, inner)))
        )
    return jnp.concatenate(
        [jnp.concatenate(top, axis=1), jnp.concatenate(bottom, axis=1)], axis=0
    )


def inverse(powers, square, tall):
    return by_lanes([by_rows(p, tall[1]) for p in powers], square[2], square[3])


def kernel(
    sizes, frames, following, square_in, tall_in, out,
    ext, rim, packed, spec, scale, result, square, tall, local_sem, send_sem, recv_sem, out_sem,
):
    F, H, B = frames.shape
    rows = H // STRIDE
    pairs = rows // 2
    tm, row, col = (lax.axis_index(a) for a in ("tm", "row", "col"))
    last_tm, last_row, last_col = (s - 1 for s in sizes)
    has_next, has_prev = tm < last_tm, tm > 0
    has_below, has_above = row < last_row, row > 0
    has_right, has_left = col < last_col, col > 0
    up, left, back = (jnp.maximum(v - 1, 0) for v in (row, col, tm))
    down, right, ahead = (
        jnp.minimum(v + 1, s) for v, s in ((row, last_row), (col, last_col), (tm, last_tm))
    )

    own = pltpu.make_async_copy(frames, ext.at[pl.ds(0, F), pl.ds(0, H), pl.ds(0, B)], local_sem.at[0])
    own.start()
    after = pltpu.make_async_copy(following, ext.at[F, pl.ds(0, H), pl.ds(0, B)], local_sem.at[1])
    pl.when(~has_next)(after.start)
    load_square = pltpu.make_async_copy(square_in, square, local_sem.at[2])
    load_square.start()
    load_tall = pltpu.make_async_copy(tall_in, tall, local_sem.at[3])
    load_tall.start()

    neighbours = [
        (has_prev, (back, row, col)),
        (has_next, (ahead, row, col)),
        (has_prev & has_left, (back, row, left)),
        (has_next & has_right, (ahead, row, right)),
        (has_prev & has_above & has_left, (back, up, left)),
        (has_next & has_below & has_right, (ahead, down, right)),
        (has_above, (tm, up, col)),
        (has_below, (tm, down, col)),
        (has_left, (tm, row, left)),
        (has_right, (tm, row, right)),
        (has_above & has_left, (tm, up, left)),
        (has_below & has_right, (tm, down, right)),
    ]
    barrier = pltpu.get_barrier_semaphore()
    for there, device in neighbours:
        @pl.when(there)
        def _(device=device):
            pl.semaphore_signal(barrier, inc=1, device_id=device, device_id_type=MESH)
    pl.semaphore_wait(barrier, sum(there.astype(jnp.int32) for there, _ in neighbours))

    def remote(source, target, number, device):
        return pltpu.make_async_remote_copy(
            src_ref=source, dst_ref=target, send_sem=send_sem.at[number],
            recv_sem=recv_sem.at[number], device_id=device, device_id_type=MESH,
        )

    edges = [0, STRIDE] + [STRIDE + W * (p + 1) for p in range(pairs - 1)] + [H]
    bands = [
        remote(
            frames.at[0, pl.ds(lo, hi - lo)], ext.at[F, pl.ds(lo, hi - lo)], n, (back, row, col)
        )
        for n, (lo, hi) in enumerate(zip(edges[:-1], edges[1:]))
    ]
    base = len(bands)
    quarter = H // 4
    cells, corner, head = pl.ds(0, quarter), pl.ds(quarter, 8), pl.ds(0, 8)
    mine = pl.ds(0, F)
    below = remote(frames.at[:, pl.ds(0, STRIDE), :], ext.at[mine, pl.ds(H, STRIDE)], base, (tm, up, col))
    below_late = remote(ext.at[F, pl.ds(0, STRIDE)], ext.at[F, pl.ds(H, STRIDE)], base + 1, (tm, up, col))
    to_side = remote(packed.at[mine], rim.at[mine, cells], base + 2, (tm, row, left))
    to_corner = remote(packed.at[mine, head], rim.at[mine, corner], base + 3, (tm, up, left))
    side_back = remote(packed.at[0], rim.at[F, cells], base + 4, (back, row, left))
    corner_back = remote(packed.at[0, head], rim.at[F, corner], base + 5, (back, up, left))
    side_end = remote(packed.at[F], rim.at[F, cells], base + 4, (tm, row, left))
    corner_end = remote(packed.at[F, head], rim.at[F, corner], base + 5, (tm, up, left))
    diagonal = has_above & has_left
    sides = [
        (has_left, to_side),
        (diagonal, to_corner),
        (has_left & has_prev, side_back),
        (diagonal & has_prev, corner_back),
    ]
    ends = [(has_left & ~has_next, side_end), (diagonal & ~has_next, corner_end)]

    @pl.when(has_prev)
    def _():
        for band in bands[:DEPTH]:
            band.start()
    pl.when(has_above)(below.start)

    own.wait()
    for f in range(F):
        packed[f] = pack(ext[f, pl.ds(0, H), pl.ds(0, LANES)])
    for goes, copy in sides:
        pl.when(goes)(copy.start)

    @pl.when(~has_next)
    def _():
        after.wait()
        packed[F] = pack(ext[F, pl.ds(0, H), pl.ds(0, LANES)])
    for goes, copy in ends:
        pl.when(goes)(copy.start)
    @pl.when(has_prev)
    def _():
        for band in bands[DEPTH:]:
            band.start()

    @pl.when(~has_right)
    def _():
        rim[...] = jnp.zeros(rim.shape, F32)

    @pl.when(~has_below)
    def _():
        ext[:, pl.ds(H, STRIDE), :] = jnp.zeros((F + 1, STRIDE, B), F32)
        rim[:, corner, :] = jnp.zeros((F + 1, 8, LANES), F32)

    load_square.wait()
    load_tall.wait()
    pl.when(has_below)(below.wait_recv)
    pl.when(has_right)(to_side.wait_recv)
    pl.when(has_right & has_below)(to_corner.wait_recv)

    def spectra(frame, p):
        blocks = []
        for r in range(2):
            start = pl.multiple_of((2 * p + r) * STRIDE, STRIDE)
            tiles = pl.ds(pl.multiple_of((2 * p + r) * 8, 8), 16)
            blocks.append(
                jnp.concatenate([ext[frame, pl.ds(start, W), :], unpack(rim[frame, tiles])], axis=1)
            )
        return forward(blocks, square, tall)

    def keep(slot, p, found):
        for r in range(2):
            spec[slot, 2 * p + r] = found[0][r]
            scale[slot, 2 * p + r] = jnp.broadcast_to(found[1][r], scale.shape[2:])

    def emit(frame, slot, p, found):
        powers = [multiply(spec[slot, 2 * p + r], found[0][r]) for r in range(2)]
        planes = inverse(powers, square, tall)
        for r in range(2):
            factor = found[1][r] * scale[slot, 2 * p + r][:1]
            result[frame, 2 * p + r] = planes[r] * factor

    def to_out(frame, p):
        part = pl.ds(2 * p, 2)
        return pltpu.make_async_copy(
            result.at[frame, part], out.at[frame, part], out_sem.at[frame, p]
        )

    for p in range(pairs):
        keep(0, p, spectra(0, p))

    for f in range(1, F):
        @pl.loop(0, pairs)
        def _(p):
            found = spectra(f, p)
            emit(f - 1, (f - 1) % 2, p, found)
            keep(f % 2, p, found)
            to_out(f - 1, p).start()

    pl.when(has_next)(bands[0].wait_recv)
    pl.when(has_above)(below_late.start)
    pl.when(has_right)(side_back.wait_recv)
    for p in range(pairs):
        pl.when(has_next)(bands[p + 1].wait_recv)
        if p == pairs - 1:
            pl.when(has_below)(below_late.wait_recv)
            pl.when(has_right & has_below)(corner_back.wait_recv)
        emit(F - 1, (F - 1) % 2, p, spectra(F, p))
        to_out(F - 1, p).start()

    @pl.when(has_prev)
    def _():
        for band in bands:
            band.wait_send()
    pl.when(has_above)(below.wait_send)
    pl.when(has_above)(below_late.wait_send)
    for goes, copy in sides + ends:
        pl.when(goes)(copy.wait_send)
    for f in range(F):
        for p in range(pairs):
            to_out(f, p).wait()


def on_device(sizes, frames, following):
    F, H, B = frames.shape
    rows, lanes = H // STRIDE, B // STRIDE * W
    square, tall = tables()
    copies = 1 + rows // 2 + 1 + 6
    return pl.pallas_call(
        functools.partial(kernel, sizes),
        out_shape=jax.ShapeDtypeStruct((F, rows, W, lanes), F32),
        in_specs=[pl.BlockSpec(memory_space=pl.ANY)] * 4,
        out_specs=pl.BlockSpec(memory_space=pl.ANY),
        scratch_shapes=[
            pltpu.VMEM((F + 1, H + STRIDE, B), F32),
            pltpu.VMEM((F + 1, H // 4 + 8, LANES), F32),
            pltpu.VMEM((F + 1, H // 4, LANES), F32),
            pltpu.VMEM((2, rows, W, lanes), F32),
            pltpu.VMEM((2, rows, 8, lanes), F32),
            pltpu.VMEM((F, rows, W, lanes), F32),
            pltpu.VMEM(square.shape, BF16),
            pltpu.VMEM(tall.shape, BF16),
            pltpu.SemaphoreType.DMA((4,)),
            pltpu.SemaphoreType.DMA((copies,)),
            pltpu.SemaphoreType.DMA((copies,)),
            pltpu.SemaphoreType.DMA((F, rows // 2)),
        ],
        compiler_params=pltpu.CompilerParams(
            collective_id=0, has_side_effects=True, vmem_limit_bytes=60 * 1024 * 1024
        ),
    )(frames, following, jnp.asarray(square), jnp.asarray(tall))


def solution(mesh):
    sizes = tuple(mesh.shape[a] for a in ("tm", "row", "col"))
    return jax.shard_map(
        functools.partial(on_device, sizes),
        mesh=mesh,
        in_specs=(P("tm", "row", "col"), P("row", "col")),
        out_specs=P("tm", "row", None, "col"),
        check_vma=False,
    )
```

```python
import functools

import jax
import jax.numpy as jnp
import ml_dtypes
import numpy as np
from jax import lax
from jax.experimental import pallas as pl
from jax.experimental.pallas import tpu as pltpu
from jax.sharding import PartitionSpec as P

W = 64
HALF = W // 2
STRIDE = 32
LANES = 128
GROUP = 256
PER = GROUP // W
DEPTH = 2
MESH = pl.DeviceIdType.MESH
BF16 = jnp.bfloat16
F32 = jnp.float32


def halves(table):
    high = table.astype(ml_dtypes.bfloat16)
    low = (table - high.astype(np.float64)).astype(ml_dtypes.bfloat16)
    return high, low


def tables():
    angle = 2 * np.pi * (np.outer(np.arange(W), np.arange(HALF + 1)) % W) / W
    cosine, sine = np.cos(angle), np.sin(angle)
    packed = np.concatenate([cosine[:, :HALF], cosine[:, HALF:], sine[:, 1:HALF]], axis=1)
    sign = np.where(np.arange(W) > HALF, -1.0, 1.0)
    weight = np.where(np.arange(W) % HALF == 0, 1.0, 2.0)
    forward_lanes = np.zeros((GROUP, GROUP))
    inverse_lanes = np.zeros((GROUP, GROUP))
    ones = np.zeros((GROUP, GROUP))
    for w in range(PER):
        cells = slice(w * W, w * W + W)
        ones[cells, cells] = 1.0
        for part in range(2):
            slots = slice(part * HALF, part * HALF + HALF)
            place = slice(part * LANES + w * HALF, part * LANES + w * HALF + HALF)
            forward_lanes[cells, place] = (packed * sign)[:, slots]
            inverse_lanes[place, cells] = (packed * weight)[:, slots].T
    square = np.stack(
        [*halves(forward_lanes), *halves(inverse_lanes), ones.astype(ml_dtypes.bfloat16)]
    )
    down, up = packed.T, packed * weight / float(W * W * W)
    tall = []
    for table in (down, up):
        high, low = halves(table)
        tall.append(np.concatenate([high, low, high, low], axis=1))
    return square, np.stack(tall)


def split(x):
    high = x.astype(BF16)
    return high, (x - high.astype(F32)).astype(BF16)


def dot(a, b):
    return jnp.dot(a, b, preferred_element_type=F32)


def pack(columns):
    lane = lax.broadcasted_iota(jnp.int32, (8, LANES), 1)
    out = []
    for top in range(0, columns.shape[0], STRIDE):
        tiles = [columns[top + 8 * b : top + 8 * b + 8] for b in range(4)]
        tile = tiles[0]
        for b in range(1, 4):
            tile = jnp.where(lane < b * STRIDE, tile, pltpu.roll(tiles[b], b * STRIDE, 1))
        out.append(tile)
    return jnp.concatenate(out, axis=0)


def unpack(packed):
    out = []
    for top in range(0, packed.shape[0], 8):
        tile = packed[top : top + 8]
        out.append(tile)
        out += [pltpu.roll(tile, LANES - b * STRIDE, 1) for b in range(1, 4)]
    return jnp.concatenate(out, axis=0)


def expand(block):
    count = block.shape[1] // LANES - 1
    lane = lax.broadcasted_iota(jnp.int32, (W, LANES), 1)
    out = []
    for n in range(count):
        here = block[:, n * LANES : (n + 1) * LANES]
        after = block[:, (n + 1) * LANES : (n + 2) * LANES]
        out.append(jnp.where(lane < W, here, pltpu.roll(here, STRIDE, 1)))
        mixed = jnp.where(lane >= LANES - STRIDE, here, after)
        out.append(
            jnp.where(lane < W, pltpu.roll(here, W, 1), pltpu.roll(mixed, LANES - STRIDE, 1))
        )
    return jnp.concatenate(out, axis=1)


def group_sums(columns, ones):
    groups = columns[0].shape[1] // GROUP
    tall = jnp.concatenate(
        [c[:, g * GROUP : (g + 1) * GROUP] for c in columns for g in range(groups)], axis=0
    )
    high, rest = tall.astype(BF16), None
    rest = tall - high.astype(F32)
    mid, low = split(rest)
    rows = tall.shape[0]
    sums = dot(jnp.concatenate([high, mid, low], axis=0), ones)
    sums = sums[:rows] + sums[rows : 2 * rows] + sums[2 * rows :]
    out = []
    for c in range(len(columns)):
        parts = [sums[(c * groups + g) * 8 : (c * groups + g) * 8 + 8] for g in range(groups)]
        out.append(jnp.sum(jnp.concatenate(parts, axis=1), axis=0, keepdims=True))
    return out


def fold(x):
    return jnp.sum(x.reshape(W // 8, 8, x.shape[1]), axis=0)


def stack_groups(arrays):
    return jnp.concatenate(
        [
            a[:, g * GROUP : (g + 1) * GROUP]
            for a in arrays
            for g in range(a.shape[1] // GROUP)
        ],
        axis=0,
    )


def unstack_groups(tall, count):
    groups = tall.shape[0] // (count * W)
    return [
        jnp.concatenate(
            [tall[(c * groups + g) * W : (c * groups + g + 1) * W] for g in range(groups)], axis=1
        )
        for c in range(count)
    ]


def by_lanes(arrays, high_table, low_table):
    high, low = split(stack_groups(arrays))
    rows = high.shape[0]
    both = dot(jnp.concatenate([high, low], axis=0), high_table)
    tall = both[:rows] + both[rows:] + dot(high, low_table)
    return unstack_groups(tall, len(arrays))


def by_rows(x, table):
    high, low = split(x)
    return dot(table, jnp.concatenate([high, high, low, low], axis=0))


def forward(blocks, square, tall):
    windows = [expand(b) for b in blocks]
    means = group_sums([fold(w) for w in windows], square[4])
    centred = [w - m * (1.0 / (W * W)) for w, m in zip(windows, means)]
    spreads = group_sums([fold(c * c) for c in centred], square[4])
    scales = [lax.rsqrt(s * (1.0 / (W * W)) + 1e-05) for s in spreads]
    rows = by_lanes(centred, square[0], square[1])
    return [by_rows(r, tall[0]) for r in rows], scales


def multiply(x1, x2):
    row = lax.broadcasted_iota(jnp.int32, (HALF, LANES), 0)
    lane = lax.broadcasted_iota(jnp.int32, (HALF, LANES), 1)
    mk = row == 0
    ml = lax.rem(lane, HALF) == 0
    either, both = mk | ml, mk & ml
    top, bottom = [], []
    for g in range(x1.shape[1] // GROUP):
        real, imag = slice(g * GROUP, g * GROUP + LANES), slice(g * GROUP + LANES, (g + 1) * GROUP)
        a1, c1, d1, b1 = x1[:HALF, real], x1[:HALF, imag], x1[HALF:, real], x1[HALF:, imag]
        a2, c2, d2, b2 = x2[:HALF, real], x2[:HALF, imag], x2[HALF:, real], x2[HALF:, imag]
        bb, cc, dd = b1 * b2, c1 * c2, d1 * d2
        cb_bc, bd_db = c1 * b2 - b1 * c2, b1 * d2 - d1 * b2
        top.append(
            a1 * a2 + jnp.where(ml, 0.0, cc) + jnp.where(mk, 0.0, dd) + jnp.where(either, 0.0, bb)
        )
        top.append(
            jnp.where(ml, cc, c1 * a2 - a1 * c2) + jnp.where(mk, 0.0, jnp.where(ml, bb, bd_db))
        )
        bottom.append(
            jnp.where(mk, dd, a1 * d2 - d1 * a2) + jnp.where(ml, 0.0, jnp.where(mk, bb, cb_bc))
        )
        inner = c1 * d2 + d1 * c2 - a1 * b2 - b1 * a2
        bottom.append(
            jnp.where(both, bb, jnp.where(ml, cb_bc, jnp.where(mk, bd_db, inner)))
        )
    return jnp.concatenate(
        [jnp.concatenate(top, axis=1), jnp.concatenate(bottom, axis=1)], axis=0
    )


def inverse(powers, square, tall):
    return by_lanes([by_rows(p, tall[1]) for p in powers], square[2], square[3])


def kernel(
    sizes, frames, following, square_in, tall_in, out,
    ext, rim, packed, spec, scale, result, square, tall, local_sem, send_sem, recv_sem, out_sem,
):
    F, H, B = frames.shape
    rows = H // STRIDE
    pairs = rows // 2
    tm, row, col = (lax.axis_index(a) for a in ("tm", "row", "col"))
    last_tm, last_row, last_col = (s - 1 for s in sizes)
    has_next, has_prev = tm < last_tm, tm > 0
    has_below, has_above = row < last_row, row > 0
    has_right, has_left = col < last_col, col > 0
    up, left, back = (jnp.maximum(v - 1, 0) for v in (row, col, tm))
    down, right, ahead = (
        jnp.minimum(v + 1, s) for v, s in ((row, last_row), (col, last_col), (tm, last_tm))
    )

    own = pltpu.make_async_copy(frames, ext.at[pl.ds(0, F), pl.ds(0, H), pl.ds(0, B)], local_sem.at[0])
    own.start()
    after = pltpu.make_async_copy(following, ext.at[F, pl.ds(0, H), pl.ds(0, B)], local_sem.at[1])
    pl.when(~has_next)(after.start)
    load_square = pltpu.make_async_copy(square_in, square, local_sem.at[2])
    load_square.start()
    load_tall = pltpu.make_async_copy(tall_in, tall, local_sem.at[3])
    load_tall.start()

    neighbours = [
        (has_prev, (back, row, col)),
        (has_next, (ahead, row, col)),
        (has_prev & has_left, (back, row, left)),
        (has_next & has_right, (ahead, row, right)),
        (has_prev & has_above & has_left, (back, up, left)),
        (has_next & has_below & has_right, (ahead, down, right)),
        (has_above, (tm, up, col)),
        (has_below, (tm, down, col)),
        (has_left, (tm, row, left)),
        (has_right, (tm, row, right)),
        (has_above & has_left, (tm, up, left)),
        (has_below & has_right, (tm, down, right)),
    ]
    barrier = pltpu.get_barrier_semaphore()
    for there, device in neighbours:
        @pl.when(there)
        def _(device=device):
            pl.semaphore_signal(barrier, inc=1, device_id=device, device_id_type=MESH)
    pl.semaphore_wait(barrier, sum(there.astype(jnp.int32) for there, _ in neighbours))

    def remote(source, target, number, device):
        return pltpu.make_async_remote_copy(
            src_ref=source, dst_ref=target, send_sem=send_sem.at[number],
            recv_sem=recv_sem.at[number], device_id=device, device_id_type=MESH,
        )

    edges = [0, STRIDE] + [STRIDE + W * (p + 1) for p in range(pairs - 1)] + [H]
    bands = [
        remote(
            frames.at[0, pl.ds(lo, hi - lo)], ext.at[F, pl.ds(lo, hi - lo)], n, (back, row, col)
        )
        for n, (lo, hi) in enumerate(zip(edges[:-1], edges[1:]))
    ]
    base = len(bands)
    quarter = H // 4
    cells, corner, head = pl.ds(0, quarter), pl.ds(quarter, 8), pl.ds(0, 8)
    mine = pl.ds(0, F)
    below = remote(frames.at[:, pl.ds(0, STRIDE), :], ext.at[mine, pl.ds(H, STRIDE)], base, (tm, up, col))
    below_late = remote(ext.at[F, pl.ds(0, STRIDE)], ext.at[F, pl.ds(H, STRIDE)], base + 1, (tm, up, col))
    to_side = remote(packed.at[mine], rim.at[mine, cells], base + 2, (tm, row, left))
    to_corner = remote(packed.at[mine, head], rim.at[mine, corner], base + 3, (tm, up, left))
    side_back = remote(packed.at[0], rim.at[F, cells], base + 4, (back, row, left))
    corner_back = remote(packed.at[0, head], rim.at[F, corner], base + 5, (back, up, left))
    side_end = remote(packed.at[F], rim.at[F, cells], base + 4, (tm, row, left))
    corner_end = remote(packed.at[F, head], rim.at[F, corner], base + 5, (tm, up, left))
    diagonal = has_above & has_left
    sides = [
        (has_left, to_side),
        (diagonal, to_corner),
        (has_left & has_prev, side_back),
        (diagonal & has_prev, corner_back),
    ]
    ends = [(has_left & ~has_next, side_end), (diagonal & ~has_next, corner_end)]

    @pl.when(has_prev)
    def _():
        for band in bands[:DEPTH]:
            band.start()
    pl.when(has_above)(below.start)

    own.wait()
    for f in range(F):
        packed[f] = pack(ext[f, pl.ds(0, H), pl.ds(0, LANES)])
    for goes, copy in sides:
        pl.when(goes)(copy.start)

    @pl.when(~has_next)
    def _():
        after.wait()
        packed[F] = pack(ext[F, pl.ds(0, H), pl.ds(0, LANES)])
    for goes, copy in ends:
        pl.when(goes)(copy.start)
    @pl.when(has_prev)
    def _():
        for band in bands[DEPTH:]:
            band.start()

    @pl.when(~has_right)
    def _():
        rim[...] = jnp.zeros(rim.shape, F32)

    @pl.when(~has_below)
    def _():
        ext[:, pl.ds(H, STRIDE), :] = jnp.zeros((F + 1, STRIDE, B), F32)
        rim[:, corner, :] = jnp.zeros((F + 1, 8, LANES), F32)

    load_square.wait()
    load_tall.wait()
    pl.when(has_below)(below.wait_recv)
    pl.when(has_right)(to_side.wait_recv)
    pl.when(has_right & has_below)(to_corner.wait_recv)

    def spectra(frame, p):
        blocks = []
        for r in range(2):
            start = pl.multiple_of((2 * p + r) * STRIDE, STRIDE)
            tiles = pl.ds(pl.multiple_of((2 * p + r) * 8, 8), 16)
            blocks.append(
                jnp.concatenate([ext[frame, pl.ds(start, W), :], unpack(rim[frame, tiles])], axis=1)
            )
        return forward(blocks, square, tall)

    def keep(slot, p, found):
        for r in range(2):
            spec[slot, 2 * p + r] = found[0][r]
            scale[slot, 2 * p + r] = jnp.broadcast_to(found[1][r], scale.shape[2:])

    def emit(frame, slot, p, found):
        powers = [multiply(spec[slot, 2 * p + r], found[0][r]) for r in range(2)]
        planes = inverse(powers, square, tall)
        for r in range(2):
            factor = found[1][r] * scale[slot, 2 * p + r][:1]
            result[frame, 2 * p + r] = planes[r] * factor

    def to_out(frame, p):
        part = pl.ds(2 * p, 2)
        return pltpu.make_async_copy(
            result.at[frame, part], out.at[frame, part], out_sem.at[frame, p]
        )

    for p in range(pairs):
        keep(0, p, spectra(0, p))

    for f in range(1, F):
        @pl.loop(0, pairs)
        def _(p):
            found = spectra(f, p)
            emit(f - 1, (f - 1) % 2, p, found)
            keep(f % 2, p, found)
            to_out(f - 1, p).start()

    pl.when(has_next)(bands[0].wait_recv)
    pl.when(has_above)(below_late.start)
    pl.when(has_right)(side_back.wait_recv)
    for p in range(pairs):
        pl.when(has_next)(bands[p + 1].wait_recv)
        if p == pairs - 1:
            pl.when(has_below)(below_late.wait_recv)
            pl.when(has_right & has_below)(corner_back.wait_recv)
        emit(F - 1, (F - 1) % 2, p, spectra(F, p))
        to_out(F - 1, p).start()

    @pl.when(has_prev)
    def _():
        for band in bands:
            band.wait_send()
    pl.when(has_above)(below.wait_send)
    pl.when(has_above)(below_late.wait_send)
    for goes, copy in sides + ends:
        pl.when(goes)(copy.wait_send)
    for f in range(F):
        for p in range(pairs):
            to_out(f, p).wait()


def on_device(sizes, frames, following):
    F, H, B = frames.shape
    rows, lanes = H // STRIDE, B // STRIDE * W
    square, tall = tables()
    copies = 1 + rows // 2 + 1 + 6
    return pl.pallas_call(
        functools.partial(kernel, sizes),
        out_shape=pltpu.VMEM((F, rows, W, lanes), F32),
        in_specs=[pl.BlockSpec(memory_space=pl.ANY)] * 4,
        out_specs=pl.BlockSpec(memory_space=pl.ANY),
        scratch_shapes=[
            pltpu.VMEM((F + 1, H + STRIDE, B), F32),
            pltpu.VMEM((F + 1, H // 4 + 8, LANES), F32),
            pltpu.VMEM((F + 1, H // 4, LANES), F32),
            pltpu.VMEM((2, rows, W, lanes), F32),
            pltpu.VMEM((2, rows, 8, lanes), F32),
            pltpu.VMEM((F, rows, W, lanes), F32),
            pltpu.VMEM(square.shape, BF16),
            pltpu.VMEM(tall.shape, BF16),
            pltpu.SemaphoreType.DMA((4,)),
            pltpu.SemaphoreType.DMA((copies,)),
            pltpu.SemaphoreType.DMA((copies,)),
            pltpu.SemaphoreType.DMA((F, rows // 2)),
        ],
        compiler_params=pltpu.CompilerParams(
            collective_id=0, has_side_effects=True, vmem_limit_bytes=58 * 1024 * 1024
        ),
    )(frames, following, jnp.asarray(square), jnp.asarray(tall))


def solution(mesh):
    sizes = tuple(mesh.shape[a] for a in ("tm", "row", "col"))
    return jax.shard_map(
        functools.partial(on_device, sizes),
        mesh=mesh,
        in_specs=(P("tm", "row", "col"), P("row", "col")),
        out_specs=P("tm", "row", None, "col"),
        check_vma=False,
    )
```
